32 devices in a mesh: scen: 2 (over x), rb: 16 (over z, y, core).
Axes of the slice: x: 2, y: 2, z: 4, core: 2. Of those that a mesh axis runs over, the one named last changes fastest.
Arguments:
- right_side: float32 [16384, 32], P(('scen', 'rb')), parts along dimension 0, may hold values from -6 to 6
- blocks: float32 [32, 8, 512, 512], P(('scen', 'rb')), parts along dimension 0, as said below
- block_cols: int32 [32, 8], P(('scen', 'rb')), parts along dimension 0, may hold values from 0 to 15, as said below
- block_counts: int32 [32], P(('scen', 'rb')), parts along dimension 0, may hold values from 1 to 8, as said below
Outputs:
- solution: float32 [16384, 32], P(('scen', 'rb')), parts along dimension 0
- residual: float32 [16384, 32], P(('scen', 'rb')), parts along dimension 0
The draws below stay inside these ranges and needn't reach their ends.
There are 2 independent parts, one for each index of `scen`. The reference program is written for one: setup_inputs(seed, part) draws one part's arguments, and reference() takes and returns one part's arrays. A program takes and returns all parts, laid end to end along the dimension named above; each array names one. Nothing has to cross between parts.
Inputs may be any that keep to these rules, and one draw needn't show every extreme that they name: `block_cols`: slot 0 of row block r holds r. For r >= 1, slots 1 to block_counts[r] - 1 hold distinct column blocks from r + 1 to r + 16, and later slots hold r. Row block 0 links to the whole matrix: its slot 1 holds 8, its slot 2 holds 15, and its slots from 3 on hold column blocks from 1 to 16, distinct among themselves. `block_counts`: row block 0 uses all 8 slots. `blocks`: slot 0 of every row block is symmetric, and the matrix assembled as in the reference program is symmetric positive definite.
All inputs are finite; a program needn't handle non-finite values.
Results may differ from the reference program's by a relative error of at most 0.0003.
Values sent between devices are 32-bit elements; how exact they have to be, the bound alone decides.
A program may use at most 64 MiB of HBM per device.

```python
import math
import jax
import jax.numpy as jnp
from jax import lax

BS = 512
NR = 32
SLOTS = 8
ITERS = 2
WINDOW = 16
ROWBLOCKS = 16
ORDER = 8192


def pattern(key):
    key = jax.random.fold_in(key, 11)
    first_key, second_key = jax.random.split(key)
    rows = jnp.arange(ROWBLOCKS, dtype=jnp.int32)
    counted = jax.random.randint(first_key, (ROWBLOCKS,), 1, SLOTS + 1).astype(jnp.int32)
    counted = jnp.minimum(counted, ROWBLOCKS - rows)
    counted = jnp.where(rows == 0, SLOTS, counted).astype(jnp.int32)
    offsets = jnp.arange(1, WINDOW + 1, dtype=jnp.int32)
    scores = jax.random.randint(second_key, (ROWBLOCKS, WINDOW), 0, 2 ** 20).astype(jnp.int32) * WINDOW + offsets[None, :] - 1
    valid = (rows[:, None] + offsets[None, :] <= ROWBLOCKS - 1).astype(jnp.int32)
    scores = scores + valid * 2 ** 26
    ranked = lax_top(scores, SLOTS - 1)
    chosen = jnp.concatenate([jnp.zeros((ROWBLOCKS, 1), jnp.int32), ranked + 1], axis=1)
    slot_ids = jnp.arange(SLOTS, dtype=jnp.int32)
    used = slot_ids[None, :] < counted[:, None]
    columns = rows[:, None] + jnp.where(used, chosen, 0)
    anchor = rows[:, None] == 0
    columns = jnp.where(anchor & (slot_ids[None, :] == 1), ROWBLOCKS // 2, columns)
    columns = jnp.where(anchor & (slot_ids[None, :] == 2), ROWBLOCKS - 1, columns)
    return (counted, columns.astype(jnp.int32))


def lax_top(scores, many):
    values, indices = jax.lax.top_k(scores, many)
    return indices.astype(jnp.int32)


def draw_block_counts(key, part):
    return pattern(key)[0]


def draw_block_cols(key, part):
    return pattern(key)[1]


def draw_blocks(key, part):
    key = jax.random.fold_in(key, 5)
    first_key, second_key = jax.random.split(key)
    sigma = 0.25 / math.sqrt(3.0 * SLOTS * BS)
    shape = (ROWBLOCKS, SLOTS, BS, BS)
    spread = sigma * math.sqrt(3.0)
    entries = jax.random.uniform(first_key, shape, jnp.float32, -spread, spread)
    diagonal = jax.random.uniform(second_key, (ROWBLOCKS, BS), jnp.float32, 1.0, 2.0)
    own = entries[:, 0]
    own = (own + jnp.swapaxes(own, 1, 2)) * math.sqrt(0.5)
    own = own + diagonal[:, :, None] * jnp.eye(BS, dtype=jnp.float32)[None, :, :]
    return jnp.concatenate([own[:, None], entries[:, 1:]], axis=1).astype(jnp.float32)


def block_scale(rng, extent, cuts, smallest, high):
    level = 1.0
    for position, shards_of in cuts:
        steps = jax.random.uniform(jax.random.fold_in(jax.random.fold_in(rng, 6), position), (shards_of,), jnp.float32, smallest / len(cuts), high / len(cuts))
        level = level * jnp.repeat(jnp.exp(steps), extent[position] // shards_of).reshape((-1,) + (1,) * (len(extent) - 1 - position))
    return level


def gaussian(stream_key, dims, scale, reach, cuts=(), kind=jnp.bfloat16):
    level = block_scale(stream_key, dims, cuts, -0.22, 0.18) if cuts else 1.0
    result = jax.random.normal(stream_key, dims, jnp.float32) * scale * level
    return jnp.minimum(jnp.maximum(result, -reach), reach).astype(kind)


def setup_inputs(seed: int = 0, part: int = 0) -> dict:
    streams_of = jax.random.split(jax.random.key(seed), 5)
    part_keys = jax.random.split(jax.random.fold_in(streams_of[4], part), 5)
    right_side = gaussian(part_keys[0], (ORDER, NR), 1.0, 6.0, ((0, 16),), jnp.float32)
    blocks = draw_blocks(jax.random.fold_in(jax.random.fold_in(streams_of[4], part), 71), part)
    block_cols = draw_block_cols(jax.random.fold_in(jax.random.fold_in(streams_of[4], part), 71), part)
    block_counts = draw_block_counts(jax.random.fold_in(jax.random.fold_in(streams_of[4], part), 71), part)
    return dict(right_side=right_side, blocks=blocks, block_cols=block_cols, block_counts=block_counts)


HIGH = lax.Precision.HIGHEST

def solve_spd(matrix, target):
    symmetric = (matrix + matrix.T) * 0.5
    factor = jnp.linalg.cholesky(symmetric)
    middle = lax.linalg.triangular_solve(factor, target, left_side=True, lower=True)
    return lax.linalg.triangular_solve(factor, middle, left_side=True, lower=True, transpose_a=True)

def gram(left, right):
    return jnp.dot(left.T.astype(jnp.float32), right.astype(jnp.float32), precision=HIGH, preferred_element_type=jnp.float32)

def apply_operator(direction, blocks, block_cols, block_counts):
    pieces = direction.reshape(ROWBLOCKS, BS, NR)
    slot_ids = jnp.arange(SLOTS)
    live_mask = (slot_ids[None, :] < block_counts[:, None]).astype(jnp.float32)
    mirror_mask = live_mask * (slot_ids[None, :] >= 1).astype(jnp.float32)
    picked = pieces[block_cols] * live_mask[:, :, None, None]
    forward = jnp.einsum('rsij,rsjk->rik', blocks, picked, precision=HIGH)
    mirrored = jnp.einsum('rsij,rik->rsjk', blocks, pieces, precision=HIGH) * mirror_mask[:, :, None, None]
    landed = jax.ops.segment_sum(mirrored.reshape(ROWBLOCKS * SLOTS, BS, NR), block_cols.reshape(-1), num_segments=ROWBLOCKS)
    return (forward + landed).reshape(ORDER, NR)

def reference(right_side, blocks, block_cols, block_counts):
    solution = jnp.zeros_like(right_side)
    residual = right_side
    direction = right_side
    norm_now = gram(residual, residual)
    for step_index in range(ITERS):
        image = apply_operator(direction, blocks, block_cols, block_counts)
        alpha = solve_spd(gram(direction, image), norm_now)
        solution = solution + jnp.dot(direction.astype(jnp.float32), alpha.astype(jnp.float32), precision=HIGH, preferred_element_type=jnp.float32)
        residual = residual - jnp.dot(image.astype(jnp.float32), alpha.astype(jnp.float32), precision=HIGH, preferred_element_type=jnp.float32)
        if step_index + 1 < ITERS:
            norm_next = gram(residual, residual)
            beta = solve_spd(norm_now, norm_next)
            direction = residual + jnp.dot(direction.astype(jnp.float32), beta.astype(jnp.float32), precision=HIGH, preferred_element_type=jnp.float32)
            norm_now = norm_next
    return (solution, residual)
```

```python
import functools

import jax
import jax.numpy as jnp
from jax import lax
from jax.experimental import pallas as pl
from jax.experimental.pallas import tpu as pltpu
from jax.sharding import PartitionSpec as P

F32 = jnp.float32
BF16 = jnp.bfloat16
HIGH = lax.Precision.HIGHEST
NN = (((1,), (0,)), ((), ()))
NT = (((1,), (1,)), ((), ()))


def exact(a, b, dims=NN):
    return lax.dot_general(a, b, dims, precision=HIGH, preferred_element_type=F32)


def fast(a, b, dims):
    return lax.dot_general(a, b, dims, preferred_element_type=F32)


def halves(x):
    hi = x.astype(BF16)
    return hi, (x - hi.astype(F32)).astype(BF16)


def stacked(x):
    hi, lo = halves(x)
    return jnp.concatenate([hi, lo], axis=0)


def pack(g):
    return jnp.concatenate([g[8 * i : 8 * i + 8] for i in range(g.shape[0] // 8)], axis=1)


def unpack(p):
    nr = p.shape[1] // 4
    return jnp.concatenate([p[:, nr * i : nr * i + nr] for i in range(4)], axis=0)


def solve_t(matrix, target):
    n = matrix.shape[0]
    work = jnp.concatenate([(matrix + matrix.T) * 0.5, target], axis=1)
    rows = lax.broadcasted_iota(jnp.int32, work.shape, 0)
    for k in range(n):
        pivot_row = work[k : k + 1, :] / work[k : k + 1, k : k + 1]
        work = jnp.where(rows == k, pivot_row, work - work[:, k : k + 1] * pivot_row)
    return work[:, n:].T


def loop(lo, hi, step):
    if hi - lo <= 4:
        for i in range(lo, hi):
            step(i)
    else:
        lax.fori_loop(lo, hi, lambda i, c: (step(i), c)[1], 0)


def kernel(
    n, ny, cols_ref, count_ref, rhs_ref, blocks_ref, out_ref,
    stage, bh, bl, gat, mir, cs, cr, ys, yr, zs, zr, acc, gp, gz,
    load_sem, gzs, gzr, gys, gyr, gcs, gcr, rcs, rcr, rys, ryr, rzs, rzr, pps, ppr, pzs, pzr,
):
    slots = blocks_ref.shape[1]
    nz = n // (2 * ny)
    plane = 2 * ny
    me = lax.axis_index("rb")
    c = lax.rem(me, 2)
    y = lax.rem(me // 2, ny)
    z = me // plane
    here = lax.rem(me, plane)

    def bid(zz, yy, cc):
        return (zz * ny + yy) * 2 + cc

    def remote(src, dst, ss, rs, dev):
        return pltpu.make_async_remote_copy(
            src_ref=src, dst_ref=dst, send_sem=ss, recv_sem=rs,
            device_id={"rb": dev}, device_id_type=pl.DeviceIdType.MESH,
        )

    def load(s):
        return pltpu.make_async_copy(blocks_ref.at[0, s], stage.at[s], load_sem.at[s])

    loop(0, slots, lambda s: load(s).start())

    barrier = pltpu.get_barrier_semaphore()

    def greet(dev):
        pl.semaphore_signal(
            barrier, inc=1, device_id={"rb": dev}, device_id_type=pl.DeviceIdType.MESH
        )

    def plane_dev(k):
        return z * plane + lax.rem(here + k, plane)

    def line_dev(k):
        return lax.rem(z + k, nz) * plane + here

    loop(1, plane, lambda k: greet(plane_dev(k)))
    loop(1, nz, lambda k: greet(line_dev(k)))

    rhs = rhs_ref[...]
    zero = jnp.zeros_like(rhs)
    for it in range(2):
        gat[it, n] = zero
    gat[0, me] = rhs
    mir[0] = zero
    pl.semaphore_wait(barrier, plane - 1 + nz - 1)

    def copy_gz(it, dz, block, dev):
        ref = gat.at[it, block]
        return remote(ref, ref, gzs.at[it, dz], gzr.at[it, dz], dev)

    def send_gz(it, dz):
        return copy_gz(it, dz, me, me - dz * plane)

    def recv_gz(it, dz):
        return copy_gz(it, dz, me + dz * plane, me)

    def copy_gy(it, dz, block):
        ref = gat.at[it, block]
        return remote(ref, ref, gys.at[it, dz], gyr.at[it, dz], bid(z, 1 - y, c))

    def copy_gc(it, dz, j, block):
        ref = gat.at[it, block]
        return remote(
            ref, ref, gcs.at[it, j * nz + dz], gcr.at[it, j * nz + dz], bid(z, y, 1 - c)
        )

    def other(yy, j):
        return yy if j == 0 else 1 - yy

    def gather_start(it):
        def step(dz):
            @pl.when(z >= dz)
            def _():
                send_gz(it, dz).start()

        loop(1, nz, step)
        if ny == 2:
            copy_gy(it, 0, me).start()
        copy_gc(it, 0, 0, me).start()

    def gather_relay_z(it):
        def step(dz):
            @pl.when(z + dz < nz)
            def _():
                recv_gz(it, dz).wait_recv()
                block = me + dz * plane
                if ny == 2:
                    copy_gy(it, dz, block).start()
                copy_gc(it, dz, 0, block).start()

        loop(1, nz, step)

    def gather_relay_y(it):
        if ny == 1:
            return

        def step(dz):
            @pl.when(z + dz < nz)
            def _():
                block = bid(z + dz, 1 - y, c)
                copy_gy(it, dz, block).wait_recv()
                copy_gc(it, dz, 1, block).start()

        loop(0, nz, step)

    def gather_finish(it):
        def step(dz):
            @pl.when(z + dz < nz)
            def _():
                for j in range(ny):
                    copy_gc(it, dz, j, bid(z + dz, other(y, j), 1 - c)).wait_recv()

        loop(0, nz, step)

    def gather_drain(it):
        def step_z(dz):
            @pl.when(z >= dz)
            def _():
                send_gz(it, dz).wait_send()

        loop(1, nz, step_z)

        def step(dz):
            @pl.when(z + dz < nz)
            def _():
                if ny == 2:
                    copy_gy(it, dz, bid(z + dz, y, c)).wait_send()
                for j in range(ny):
                    copy_gc(it, dz, j, bid(z + dz, other(y, j), c)).wait_send()

        loop(0, nz, step)

    count = count_ref[0]
    cols = [cols_ref[0, s] for s in range(slots)]
    live = [jnp.int32(s) < count for s in range(slots)]

    def spread(target):
        first = jnp.int32(0)
        for s in (1, 2):
            first = jnp.where(live[s] & (cols[s] == target), s, first)
        second = jnp.int32(0)
        for s in range(3, slots):
            second = jnp.where(live[s] & (cols[s] == target), s, second)
        return mir[first] + mir[second]

    def copy_rc(it, dz):
        return remote(
            cs.at[it, dz], cr.at[it, dz], rcs.at[it, dz], rcr.at[it, dz], bid(z, y, 1 - c)
        )

    def copy_ry(it, dz):
        return remote(
            ys.at[it, dz], yr.at[it, dz], rys.at[it, dz], ryr.at[it, dz], bid(z, 1 - y, c)
        )

    def copy_rz(it, dz, dev):
        return remote(zs.at[it, dz], zr.at[it, dz], rzs.at[it, dz], rzr.at[it, dz], dev)

    def far_first(step):
        loop(1, nz, step)
        step(0)

    def reduce_core(it):
        def step(dz):
            @pl.when(z + dz < nz)
            def _():
                for yy in range(ny):
                    cs[it, dz, yy] = spread(bid(z + dz, yy, 1 - c))
                copy_rc(it, dz).start()

        far_first(step)

    def reduce_y(it):
        def step(dz):
            @pl.when(z + dz < nz)
            def _():
                copy_rc(it, dz).wait_recv()
                if ny == 2:
                    ys[it, dz] = spread(bid(z + dz, 1 - y, c)) + cr[it, dz, 1 - y]
                    copy_ry(it, dz).start()

        far_first(step)

    def reduce_z(it):
        def part(dz):
            mine = spread(bid(z + dz, y, c)) + cr[it, dz, y]
            if ny == 2:
                copy_ry(it, dz).wait_recv()
                mine = mine + yr[it, dz]
            return mine

        def step(dz):
            @pl.when(z + dz < nz)
            def _():
                zs[it, dz] = part(dz)
                copy_rz(it, dz, me + dz * plane).start()

        loop(1, nz, step)
        acc[...] = part(0)

    def reduce_finish(it):
        def step(dz):
            @pl.when(z >= dz)
            def _():
                copy_rz(it, dz, me).wait_recv()
                acc[...] += zr[it, dz]

        loop(1, nz, step)
        return acc[...]

    def reduce_drain(it):
        def step(dz):
            @pl.when(z + dz < nz)
            def _():
                copy_rc(it, dz).wait_send()
                if ny == 2:
                    copy_ry(it, dz).wait_send()

        loop(0, nz, step)

        def step_z(dz):
            @pl.when(z + dz < nz)
            def _():
                copy_rz(it, dz, me).wait_send()

        loop(1, nz, step_z)

    def copy_pp(i, k, slot, dev):
        ref = gp.at[i, slot]
        return remote(ref, ref, pps.at[i, k], ppr.at[i, k], dev)

    def copy_pz(i, k, slot, dev):
        ref = gz.at[i, slot]
        return remote(ref, ref, pzs.at[i, k], pzr.at[i, k], dev)

    def sum_start(i, value):
        gp[i, here] = value
        loop(1, plane, lambda k: copy_pp(i, k, here, plane_dev(k)).start())

    def sum_middle(i):
        loop(
            1, plane,
            lambda k: copy_pp(i, k, lax.rem(here - k + plane, plane), plane_dev(k)).wait_recv(),
        )
        total = gp[i, 0]
        for k in range(1, plane):
            total = total + gp[i, k]
        gz[i, z] = total
        loop(1, nz, lambda k: copy_pz(i, k, z, line_dev(k)).start())

    def sum_finish(i):
        loop(
            1, nz,
            lambda k: copy_pz(i, k, lax.rem(z - k + nz, nz), line_dev(k)).wait_recv(),
        )
        total = gz[i, 0]
        for k in range(1, nz):
            total = total + gz[i, k]
        return total

    def sum_drain(i):
        loop(1, plane, lambda k: copy_pp(i, k, here, plane_dev(k)).wait_send())
        loop(1, nz, lambda k: copy_pz(i, k, z, line_dev(k)).wait_send())

    nr = rhs.shape[0]

    def product(x2, s, dims):
        both = fast(x2, bh[s], dims)
        return both[:nr] + both[nr:] + fast(x2[:nr], bl[s], dims)

    def split_block(s):
        load(s).wait()
        hi, lo = halves(stage[s])
        bh[s] = hi
        bl[s] = lo

    def mirror(x2, lo, hi):
        def step(s, carry):
            mir[s] = product(x2, s, NN)
            return carry

        lax.fori_loop(lo, hi, step, 0)

    def forward(it):
        def step(s, total):
            col = jnp.where(s < count, cols_ref[0, s], n)
            return total + product(stacked(gat[it, col]), s, NT)

        return lax.fori_loop(1, slots, step, zero)

    def operator(it, x, first):
        x2 = stacked(x)

        if first:
            def step(s, carry):
                split_block(s)
                mir[s] = product(x2, s, NN)
                return carry

            lax.fori_loop(1, slots // 2, step, 0)
            gather_relay_z(it)
            lax.fori_loop(slots // 2, slots, step, 0)
            split_block(0)
        else:
            mirror(x2, 1, slots // 2)
            gather_relay_z(it)
            mirror(x2, slots // 2, slots)
        reduce_core(it)
        gather_relay_y(it)
        reduce_y(it)
        own = product(x2, 0, NT)
        gather_finish(it)
        return own

    packed_zero = jnp.zeros((8, 4 * nr), F32)

    gather_start(0)
    own0 = operator(0, rhs, True)
    fwd0 = forward(0)
    curved = exact(rhs, own0 + fwd0, NT) + exact(fwd0, rhs, NT)
    sum_start(0, jnp.concatenate([pack(curved), pack(exact(rhs, rhs, NT))], axis=0))
    reduce_z(0)
    sum_middle(0)
    sums = sum_finish(0)
    norm0 = unpack(sums[8:])
    alpha = solve_t(unpack(sums[:8]), norm0)
    image0 = own0 + fwd0 + reduce_finish(0)
    residual = rhs - exact(alpha, image0)
    gat[1, me] = residual
    gather_start(1)
    sum_start(1, jnp.concatenate([pack(exact(residual, residual, NT)), packed_zero], axis=0))
    solution_t = exact(alpha, rhs)

    sum_middle(1)
    own1 = operator(1, residual, False)
    norm1 = unpack(sum_finish(1)[:8])
    beta = solve_t(norm0, norm1)
    fwd1 = forward(1)
    direction = residual + exact(beta, rhs)
    fwd_d = fwd1 + exact(beta, fwd0)
    own_d = own1 + exact(beta, own0)
    curved = exact(direction, own_d + fwd_d, NT) + exact(fwd_d, direction, NT)
    sum_start(2, jnp.concatenate([pack(curved), packed_zero], axis=0))
    reduce_z(1)
    sum_middle(2)
    alpha = solve_t(unpack(sum_finish(2)[:8]), norm1)
    image = own1 + fwd1 + reduce_finish(1) + exact(beta, image0)
    out_ref[0] = solution_t + exact(alpha, direction)
    out_ref[1] = residual - exact(alpha, image)

    for it in range(2):
        gather_drain(it)
        reduce_drain(it)
    for i in range(3):
        sum_drain(i)


def body(n, ny, right_side, blocks, block_cols, block_counts):
    width, nr = right_side.shape
    slots = blocks.shape[1]
    nz = n // (2 * ny)
    dma = pltpu.SemaphoreType.DMA
    vec = (nr, width)
    out = pl.pallas_call(
        functools.partial(kernel, n, ny),
        out_shape=jax.ShapeDtypeStruct((2,) + vec, F32),
        in_specs=[
            pl.BlockSpec(memory_space=pltpu.SMEM),
            pl.BlockSpec(memory_space=pltpu.SMEM),
            pl.BlockSpec(memory_space=pltpu.VMEM),
            pl.BlockSpec(memory_space=pl.ANY),
        ],
        out_specs=pl.BlockSpec(memory_space=pltpu.VMEM),
        scratch_shapes=[
            pltpu.VMEM((slots, width, width), F32),
            pltpu.VMEM((slots, width, width), BF16),
            pltpu.VMEM((slots, width, width), BF16),
            pltpu.VMEM((2, n + 1) + vec, F32),
            pltpu.VMEM((slots,) + vec, F32),
            pltpu.VMEM((2, nz, ny) + vec, F32),
            pltpu.VMEM((2, nz, ny) + vec, F32),
            pltpu.VMEM((2, nz if ny == 2 else 1) + vec, F32),
            pltpu.VMEM((2, nz if ny == 2 else 1) + vec, F32),
            pltpu.VMEM((2, nz) + vec, F32),
            pltpu.VMEM((2, nz) + vec, F32),
            pltpu.VMEM(vec, F32),
            pltpu.VMEM((3, 2 * ny, 16, 4 * nr), F32),
            pltpu.VMEM((3, nz, 16, 4 * nr), F32),
            dma((slots,)),
            dma((2, nz)), dma((2, nz)),
            dma((2, nz if ny == 2 else 1)), dma((2, nz if ny == 2 else 1)),
            dma((2, nz * ny)), dma((2, nz * ny)),
            dma((2, nz)), dma((2, nz)),
            dma((2, nz if ny == 2 else 1)), dma((2, nz if ny == 2 else 1)),
            dma((2, nz)), dma((2, nz)),
            dma((3, 2 * ny)), dma((3, 2 * ny)),
            dma((3, nz)), dma((3, nz)),
        ],
        compiler_params=pltpu.CompilerParams(
            collective_id=0, has_side_effects=True, vmem_limit_bytes=58 * 2**20
        ),
    )(block_cols, block_counts, right_side.T, blocks)
    return out[0].T, out[1].T


def solution(mesh):
    in_specs = (
        P(("scen", "rb"), None),
        P(("scen", "rb"), None, None, None),
        P(("scen", "rb"), None),
        P(("scen", "rb")),
    )
    out_specs = (P(("scen", "rb"), None), P(("scen", "rb"), None))
    ny = max(1, 4 // mesh.shape["scen"])
    step = functools.partial(body, mesh.shape["rb"], ny)
    return jax.shard_map(step, mesh=mesh, in_specs=in_specs, out_specs=out_specs, check_vma=False)
```

```python
import functools

import jax
import jax.numpy as jnp
from jax import lax
from jax.experimental import pallas as pl
from jax.experimental.pallas import tpu as pltpu
from jax.sharding import PartitionSpec as P

F32 = jnp.float32
BF16 = jnp.bfloat16
HIGH = lax.Precision.HIGHEST
NN = (((1,), (0,)), ((), ()))
NT = (((1,), (1,)), ((), ()))


def exact(a, b, dims=NN):
    return lax.dot_general(a, b, dims, precision=HIGH, preferred_element_type=F32)


def fast(a, b, dims):
    return lax.dot_general(a, b, dims, preferred_element_type=F32)


def halves(x):
    hi = x.astype(BF16)
    return hi, (x - hi.astype(F32)).astype(BF16)


def stacked(x):
    hi, lo = halves(x)
    return jnp.concatenate([hi, lo], axis=0)


def pack(g):
    return jnp.concatenate([g[8 * i : 8 * i + 8] for i in range(g.shape[0] // 8)], axis=1)


def unpack(p):
    nr = p.shape[1] // 4
    return jnp.concatenate([p[:, nr * i : nr * i + nr] for i in range(4)], axis=0)


def solve_t(matrix, target):
    n = matrix.shape[0]
    work = jnp.concatenate([(matrix + matrix.T) * 0.5, target], axis=1)
    rows = lax.broadcasted_iota(jnp.int32, work.shape, 0)
    wide = (1, work.shape[1])
    for k in range(0, n, 4):
        span = range(4)
        row = [work[k + i : k + i + 1, :] for i in span]
        entry = [
            [jnp.broadcast_to(row[i][:, k + j : k + j + 1], wide) for j in span] for i in span
        ]
        for p in span:
            inverse = 1.0 / entry[p][p]
            row[p] = row[p] * inverse
            for j in range(p + 1, 4):
                entry[p][j] = entry[p][j] * inverse
            for i in span:
                if i != p:
                    row[i] = row[i] - entry[i][p] * row[p]
                    for j in range(p + 1, 4):
                        entry[i][j] = entry[i][j] - entry[i][p] * entry[p][j]
        swept = work
        for p in span:
            swept = swept - work[:, k + p : k + p + 1] * row[p]
        for p in span:
            swept = jnp.where(rows == k + p, row[p], swept)
        work = swept
    return work[:, n:].T


def loop(lo, hi, step):
    if hi - lo <= 16:
        for i in range(lo, hi):
            step(i)
    else:
        lax.fori_loop(lo, hi, lambda i, c: (step(i), c)[1], 0)


def kernel(
    n, ny, cols_ref, count_ref, rhs_ref, blocks_ref, out_ref,
    stage, bh, bl, gat, mir, cs, cr, ys, yr, zs, zr, acc, gp,
    load_sem, gzs, gzr, gys, gyr, gcs, gcr, rcs, rcr, rys, ryr, rzs, rzr, pps, ppr,
):
    slots = blocks_ref.shape[1]
    nz = n // (2 * ny)
    plane = 2 * ny
    me = lax.axis_index("rb")
    c = lax.rem(me, 2)
    y = lax.rem(me // 2, ny)
    z = me // plane

    def bid(zz, yy, cc):
        return (zz * ny + yy) * 2 + cc

    def remote(src, dst, ss, rs, dev):
        return pltpu.make_async_remote_copy(
            src_ref=src, dst_ref=dst, send_sem=ss, recv_sem=rs,
            device_id={"rb": dev}, device_id_type=pl.DeviceIdType.MESH,
        )

    def load(s):
        return pltpu.make_async_copy(blocks_ref.at[0, s], stage.at[s], load_sem.at[s])

    barrier = pltpu.get_barrier_semaphore()

    def peer(k):
        return lax.rem(me + k, n)

    def greet(k):
        pl.semaphore_signal(
            barrier, inc=1, device_id={"rb": peer(k)}, device_id_type=pl.DeviceIdType.MESH
        )

    loop(1, n, greet)
    loop(0, slots, lambda s: load(s).start())

    rhs = rhs_ref[...]
    zero = jnp.zeros_like(rhs)
    for it in range(2):
        gat[it, n] = zero
    gat[0, me] = rhs
    mir[0] = zero

    def copy_gz(it, dz, block, dev):
        ref = gat.at[it, block]
        return remote(ref, ref, gzs.at[it, dz], gzr.at[it, dz], dev)

    def send_gz(it, dz):
        return copy_gz(it, dz, me, me - dz * plane)

    def recv_gz(it, dz):
        return copy_gz(it, dz, me + dz * plane, me)

    def copy_gy(it, dz, block):
        ref = gat.at[it, block]
        return remote(ref, ref, gys.at[it, dz], gyr.at[it, dz], bid(z, 1 - y, c))

    def copy_gc(it, dz, j, block):
        ref = gat.at[it, block]
        return remote(
            ref, ref, gcs.at[it, j * nz + dz], gcr.at[it, j * nz + dz], bid(z, y, 1 - c)
        )

    def other(yy, j):
        return yy if j == 0 else 1 - yy

    def gather_start(it):
        def step(dz):
            @pl.when(z >= dz)
            def _():
                send_gz(it, dz).start()

        loop(1, nz, step)
        if ny == 2:
            copy_gy(it, 0, me).start()
        copy_gc(it, 0, 0, me).start()

    def gather_relay_z(it):
        def step(dz):
            @pl.when(z + dz < nz)
            def _():
                recv_gz(it, dz).wait_recv()
                block = me + dz * plane
                if ny == 2:
                    copy_gy(it, dz, block).start()
                copy_gc(it, dz, 0, block).start()

        loop(1, nz, step)

    def gather_relay_y(it):
        if ny == 1:
            return

        def step(dz):
            @pl.when(z + dz < nz)
            def _():
                block = bid(z + dz, 1 - y, c)
                copy_gy(it, dz, block).wait_recv()
                copy_gc(it, dz, 1, block).start()

        loop(0, nz, step)

    def gather_finish(it):
        def step(dz):
            @pl.when(z + dz < nz)
            def _():
                for j in range(ny):
                    copy_gc(it, dz, j, bid(z + dz, other(y, j), 1 - c)).wait_recv()

        loop(0, nz, step)

    def gather_drain(it):
        def step_z(dz):
            @pl.when(z >= dz)
            def _():
                send_gz(it, dz).wait_send()

        loop(1, nz, step_z)

        def step(dz):
            @pl.when(z + dz < nz)
            def _():
                if ny == 2:
                    copy_gy(it, dz, bid(z + dz, y, c)).wait_send()
                for j in range(ny):
                    copy_gc(it, dz, j, bid(z + dz, other(y, j), c)).wait_send()

        loop(0, nz, step)

    count = count_ref[0]
    cols = [cols_ref[0, s] for s in range(slots)]
    live = [jnp.int32(s) < count for s in range(slots)]

    def spread(target):
        first = jnp.int32(0)
        for s in (1, 2):
            first = jnp.where(live[s] & (cols[s] == target), s, first)
        second = jnp.int32(0)
        for s in range(3, slots):
            second = jnp.where(live[s] & (cols[s] == target), s, second)
        return mir[first] + mir[second]

    def copy_rc(it, dz):
        return remote(
            cs.at[it, dz], cr.at[it, dz], rcs.at[it, dz], rcr.at[it, dz], bid(z, y, 1 - c)
        )

    def copy_ry(it, dz):
        return remote(
            ys.at[it, dz], yr.at[it, dz], rys.at[it, dz], ryr.at[it, dz], bid(z, 1 - y, c)
        )

    def copy_rz(it, dz, dev):
        return remote(zs.at[it, dz], zr.at[it, dz], rzs.at[it, dz], rzr.at[it, dz], dev)

    def far_first(step):
        loop(1, nz, step)
        step(0)

    def reduce_core(it):
        def step(dz):
            @pl.when(z + dz < nz)
            def _():
                for yy in range(ny):
                    cs[it, dz, yy] = spread(bid(z + dz, yy, 1 - c))
                copy_rc(it, dz).start()

        far_first(step)

    def reduce_y(it):
        def step(dz):
            @pl.when(z + dz < nz)
            def _():
                copy_rc(it, dz).wait_recv()
                if ny == 2:
                    ys[it, dz] = spread(bid(z + dz, 1 - y, c)) + cr[it, dz, 1 - y]
                    copy_ry(it, dz).start()

        far_first(step)

    def reduce_z(it):
        def part(dz):
            mine = spread(bid(z + dz, y, c)) + cr[it, dz, y]
            if ny == 2:
                copy_ry(it, dz).wait_recv()
                mine = mine + yr[it, dz]
            return mine

        def step(dz):
            @pl.when(z + dz < nz)
            def _():
                zs[it, dz] = part(dz)
                copy_rz(it, dz, me + dz * plane).start()

        loop(1, nz, step)
        acc[...] = part(0)

    def reduce_finish(it):
        def step(dz):
            @pl.when(z >= dz)
            def _():
                copy_rz(it, dz, me).wait_recv()
                acc[...] += zr[it, dz]

        loop(1, nz, step)
        return acc[...]

    def reduce_drain(it):
        def step(dz):
            @pl.when(z + dz < nz)
            def _():
                copy_rc(it, dz).wait_send()
                if ny == 2:
                    copy_ry(it, dz).wait_send()

        loop(0, nz, step)

        def step_z(dz):
            @pl.when(z + dz < nz)
            def _():
                copy_rz(it, dz, me).wait_send()

        loop(1, nz, step_z)

    def copy_pp(i, k, slot, dev):
        ref = gp.at[i, slot]
        return remote(ref, ref, pps.at[i, k], ppr.at[i, k], dev)

    def sum_start(i, value):
        gp[i, me] = pack(value)
        loop(1, n, lambda k: copy_pp(i, k, me, peer(k)).start())

    def sum_finish(i):
        loop(1, n, lambda k: copy_pp(i, k, lax.rem(me - k + n, n), peer(k)).wait_recv())
        return unpack(jnp.sum(gp[i], axis=0))

    def sum_drain(i):
        loop(1, n, lambda k: copy_pp(i, k, me, peer(k)).wait_send())

    nr = rhs.shape[0]

    def product(x2, s, dims):
        both = fast(x2, bh[s], dims)
        return both[:nr] + both[nr:] + fast(x2[:nr], bl[s], dims)

    def split_block(s):
        load(s).wait()
        hi, lo = halves(stage[s])
        bh[s] = hi
        bl[s] = lo

    def mirror(x2, lo, hi):
        def step(s, carry):
            mir[s] = product(x2, s, NN)
            return carry

        lax.fori_loop(lo, hi, step, 0)

    def forward(it):
        def step(s, total):
            col = jnp.where(s < count, cols_ref[0, s], n)
            return total + product(stacked(gat[it, col]), s, NT)

        return lax.fori_loop(1, slots, step, zero)

    norm_part = exact(rhs, rhs, NT)
    pair = stacked(rhs)
    pl.semaphore_wait(barrier, n - 1)
    gather_start(0)
    sum_start(0, norm_part)

    def split_mirror(s, carry):
        split_block(s)
        mir[s] = product(pair, s, NN)
        return carry

    lax.fori_loop(1, slots // 2, split_mirror, 0)
    gather_relay_z(0)
    lax.fori_loop(slots // 2, slots, split_mirror, 0)
    split_block(0)
    own0 = product(pair, 0, NT)
    gather_relay_y(0)
    reduce_core(0)
    reduce_y(0)
    gather_finish(0)
    fwd0 = forward(0)
    sum_start(1, exact(rhs, own0 + fwd0, NT) + exact(fwd0, rhs, NT))
    reduce_z(0)
    norm0 = sum_finish(0)
    alpha = solve_t(sum_finish(1), norm0)
    image0 = own0 + fwd0 + reduce_finish(0)
    residual = rhs - exact(alpha, image0)
    gat[1, me] = residual
    gather_start(1)
    sum_start(2, exact(residual, residual, NT))
    solution_t = exact(alpha, rhs)

    pair = stacked(residual)
    mirror(pair, 1, slots // 2)
    gather_relay_z(1)
    mirror(pair, slots // 2, slots)
    own1 = product(pair, 0, NT)
    norm1 = sum_finish(2)
    beta = solve_t(norm0, norm1)
    gather_relay_y(1)
    reduce_core(1)
    reduce_y(1)
    direction = residual + exact(beta, rhs)
    own_d = own1 + exact(beta, own0)
    turned0 = exact(beta, fwd0)
    image_d = own1 + exact(beta, image0)
    gather_finish(1)
    fwd1 = forward(1)
    fwd_d = fwd1 + turned0
    sum_start(3, exact(direction, own_d + fwd_d, NT) + exact(fwd_d, direction, NT))
    reduce_z(1)
    alpha = solve_t(sum_finish(3), norm1)
    image = image_d + fwd1 + reduce_finish(1)
    out_ref[0] = solution_t + exact(alpha, direction)
    out_ref[1] = residual - exact(alpha, image)

    for it in range(2):
        gather_drain(it)
        reduce_drain(it)
    for i in range(4):
        sum_drain(i)


def body(n, ny, right_side, blocks, block_cols, block_counts):
    width, nr = right_side.shape
    slots = blocks.shape[1]
    nz = n // (2 * ny)
    dma = pltpu.SemaphoreType.DMA
    vec = (nr, width)
    out = pl.pallas_call(
        functools.partial(kernel, n, ny),
        out_shape=jax.ShapeDtypeStruct((2,) + vec, F32),
        in_specs=[
            pl.BlockSpec(memory_space=pltpu.SMEM),
            pl.BlockSpec(memory_space=pltpu.SMEM),
            pl.BlockSpec(memory_space=pltpu.VMEM),
            pl.BlockSpec(memory_space=pl.ANY),
        ],
        out_specs=pl.BlockSpec(memory_space=pltpu.VMEM),
        scratch_shapes=[
            pltpu.VMEM((slots, width, width), F32),
            pltpu.VMEM((slots, width, width), BF16),
            pltpu.VMEM((slots, width, width), BF16),
            pltpu.VMEM((2, n + 1) + vec, F32),
            pltpu.VMEM((slots,) + vec, F32),
            pltpu.VMEM((2, nz, ny) + vec, F32),
            pltpu.VMEM((2, nz, ny) + vec, F32),
            pltpu.VMEM((2, nz if ny == 2 else 1) + vec, F32),
            pltpu.VMEM((2, nz if ny == 2 else 1) + vec, F32),
            pltpu.VMEM((2, nz) + vec, F32),
            pltpu.VMEM((2, nz) + vec, F32),
            pltpu.VMEM(vec, F32),
            pltpu.VMEM((4, n, 8, 4 * nr), F32),
            dma((slots,)),
            dma((2, nz)), dma((2, nz)),
            dma((2, nz if ny == 2 else 1)), dma((2, nz if ny == 2 else 1)),
            dma((2, nz * ny)), dma((2, nz * ny)),
            dma((2, nz)), dma((2, nz)),
            dma((2, nz if ny == 2 else 1)), dma((2, nz if ny == 2 else 1)),
            dma((2, nz)), dma((2, nz)),
            dma((4, n)), dma((4, n)),
        ],
        compiler_params=pltpu.CompilerParams(
            collective_id=0, has_side_effects=True, vmem_limit_bytes=58 * 2**20
        ),
    )(block_cols, block_counts, right_side.T, blocks)
    return out[0].T, out[1].T


def solution(mesh):
    in_specs = (
        P(("scen", "rb"), None),
        P(("scen", "rb"), None, None, None),
        P(("scen", "rb"), None),
        P(("scen", "rb")),
    )
    out_specs = (P(("scen", "rb"), None), P(("scen", "rb"), None))
    ny = max(1, 4 // mesh.shape["scen"])
    step = functools.partial(body, mesh.shape["rb"], ny)
    return jax.shard_map(step, mesh=mesh, in_specs=in_specs, out_specs=out_specs, check_vma=False)
```

```python
import functools

import jax
import jax.numpy as jnp
from jax import lax
from jax.experimental import pallas as pl
from jax.experimental.pallas import tpu as pltpu
from jax.sharding import PartitionSpec as P

F32 = jnp.float32
BF16 = jnp.bfloat16
HIGH = lax.Precision.HIGHEST
NN = (((1,), (0,)), ((), ()))
NT = (((1,), (1,)), ((), ()))


def exact(a, b, dims=NN):
    return lax.dot_general(a, b, dims, precision=HIGH, preferred_element_type=F32)


def fast(a, b, dims):
    return lax.dot_general(a, b, dims, preferred_element_type=F32)


def halves(x):
    hi = x.astype(BF16)
    return hi, (x - hi.astype(F32)).astype(BF16)


def stacked(x):
    hi, lo = halves(x)
    return jnp.concatenate([hi, lo], axis=0)


def pack(g):
    return jnp.concatenate([g[8 * i : 8 * i + 8] for i in range(g.shape[0] // 8)], axis=1)


def unpack(p):
    nr = p.shape[1] // 4
    return jnp.concatenate([p[:, nr * i : nr * i + nr] for i in range(4)], axis=0)


def solve_t(matrix, target):
    n = matrix.shape[0]
    work = jnp.concatenate([(matrix + matrix.T) * 0.5, target], axis=1)
    rows = lax.broadcasted_iota(jnp.int32, work.shape, 0)
    wide = (1, work.shape[1])
    for k in range(0, n, 4):
        span = range(4)
        row = [work[k + i : k + i + 1, :] for i in span]
        entry = [
            [jnp.broadcast_to(row[i][:, k + j : k + j + 1], wide) for j in span] for i in span
        ]
        for p in span:
            inverse = 1.0 / entry[p][p]
            row[p] = row[p] * inverse
            for j in range(p + 1, 4):
                entry[p][j] = entry[p][j] * inverse
            for i in span:
                if i != p:
                    row[i] = row[i] - entry[i][p] * row[p]
                    for j in range(p + 1, 4):
                        entry[i][j] = entry[i][j] - entry[i][p] * entry[p][j]
        swept = work
        for p in span:
            swept = swept - work[:, k + p : k + p + 1] * row[p]
        for p in span:
            swept = jnp.where(rows == k + p, row[p], swept)
        work = swept
    return work[:, n:].T


def loop(lo, hi, step):
    if hi - lo <= 16:
        for i in range(lo, hi):
            step(i)
    else:
        lax.fori_loop(lo, hi, lambda i, c: (step(i), c)[1], 0)


def kernel(
    n, ny, cols_ref, count_ref, rhs_ref, blocks_ref, out_ref,
    stage, bh, bl, gat, mir, cs, cr, ys, yr, zs, zr, acc, gp,
    load_sem, gzs, gzr, gys, gyr, gcs, gcr, rcs, rcr, rys, ryr, rzs, rzr, pps, ppr,
):
    slots = blocks_ref.shape[1]
    nz = n // (2 * ny)
    plane = 2 * ny
    me = lax.axis_index("rb")
    c = lax.rem(me, 2)
    y = lax.rem(me // 2, ny)
    z = me // plane

    def bid(zz, yy, cc):
        return (zz * ny + yy) * 2 + cc

    def remote(src, dst, ss, rs, dev):
        return pltpu.make_async_remote_copy(
            src_ref=src, dst_ref=dst, send_sem=ss, recv_sem=rs,
            device_id={"rb": dev}, device_id_type=pl.DeviceIdType.MESH,
        )

    def load(s):
        return pltpu.make_async_copy(blocks_ref.at[0, s], stage.at[s], load_sem.at[s])

    barrier = pltpu.get_barrier_semaphore()

    def peer(k):
        return lax.rem(me + k, n)

    def greet(k):
        pl.semaphore_signal(
            barrier, inc=1, device_id={"rb": peer(k)}, device_id_type=pl.DeviceIdType.MESH
        )

    loop(1, n, greet)
    loop(0, slots, lambda s: load(s).start())

    rhs = rhs_ref[...]
    zero = jnp.zeros_like(rhs)
    for it in range(2):
        gat[it, n] = zero
    gat[0, me] = rhs
    mir[0] = zero

    def copy_gz(it, dz, block, dev):
        ref = gat.at[it, block]
        return remote(ref, ref, gzs.at[it, dz], gzr.at[it, dz], dev)

    def send_gz(it, dz):
        return copy_gz(it, dz, me, me - dz * plane)

    def recv_gz(it, dz):
        return copy_gz(it, dz, me + dz * plane, me)

    def copy_gy(it, dz, block):
        ref = gat.at[it, block]
        return remote(ref, ref, gys.at[it, dz], gyr.at[it, dz], bid(z, 1 - y, c))

    def copy_gc(it, dz, j, block):
        ref = gat.at[it, block]
        return remote(
            ref, ref, gcs.at[it, j * nz + dz], gcr.at[it, j * nz + dz], bid(z, y, 1 - c)
        )

    def other(yy, j):
        return yy if j == 0 else 1 - yy

    def gather_start(it):
        def step(dz):
            @pl.when(z >= dz)
            def _():
                send_gz(it, dz).start()

        loop(1, nz, lambda k: step(nz - k))
        if ny == 2:
            copy_gy(it, 0, me).start()
        copy_gc(it, 0, 0, me).start()

    def gather_relay_z(it, dz):
        @pl.when(z + dz < nz)
        def _():
            recv_gz(it, dz).wait_recv()
            block = me + dz * plane
            if ny == 2:
                copy_gy(it, dz, block).start()
            copy_gc(it, dz, 0, block).start()

    def gather_relay_y(it):
        if ny == 1:
            return

        def step(dz):
            @pl.when(z + dz < nz)
            def _():
                block = bid(z + dz, 1 - y, c)
                copy_gy(it, dz, block).wait_recv()
                copy_gc(it, dz, 1, block).start()

        loop(0, nz, step)

    def gather_finish(it):
        def step(dz):
            @pl.when(z + dz < nz)
            def _():
                for j in range(ny):
                    copy_gc(it, dz, j, bid(z + dz, other(y, j), 1 - c)).wait_recv()

        loop(0, nz, step)

    def gather_drain(it):
        def step_z(dz):
            @pl.when(z >= dz)
            def _():
                send_gz(it, dz).wait_send()

        loop(1, nz, step_z)

        def step(dz):
            @pl.when(z + dz < nz)
            def _():
                if ny == 2:
                    copy_gy(it, dz, bid(z + dz, y, c)).wait_send()
                for j in range(ny):
                    copy_gc(it, dz, j, bid(z + dz, other(y, j), c)).wait_send()

        loop(0, nz, step)

    count = count_ref[0]
    cols = [cols_ref[0, s] for s in range(slots)]
    live = [jnp.int32(s) < count for s in range(slots)]

    def spread(target):
        first = jnp.int32(0)
        for s in (1, 2):
            first = jnp.where(live[s] & (cols[s] == target), s, first)
        second = jnp.int32(0)
        for s in range(3, slots):
            second = jnp.where(live[s] & (cols[s] == target), s, second)
        return mir[first] + mir[second]

    def copy_rc(it, dz):
        return remote(
            cs.at[it, dz], cr.at[it, dz], rcs.at[it, dz], rcr.at[it, dz], bid(z, y, 1 - c)
        )

    def copy_ry(it, dz):
        return remote(
            ys.at[it, dz], yr.at[it, dz], rys.at[it, dz], ryr.at[it, dz], bid(z, 1 - y, c)
        )

    def copy_rz(it, dz, dev):
        return remote(zs.at[it, dz], zr.at[it, dz], rzs.at[it, dz], rzr.at[it, dz], dev)

    def far_first(step):
        loop(1, nz, step)
        step(0)

    def reduce_core(it):
        def step(dz):
            @pl.when(z + dz < nz)
            def _():
                for yy in range(ny):
                    cs[it, dz, yy] = spread(bid(z + dz, yy, 1 - c))
                copy_rc(it, dz).start()

        far_first(step)

    def reduce_y(it):
        def step(dz):
            @pl.when(z + dz < nz)
            def _():
                copy_rc(it, dz).wait_recv()
                if ny == 2:
                    ys[it, dz] = spread(bid(z + dz, 1 - y, c)) + cr[it, dz, 1 - y]
                    copy_ry(it, dz).start()

        far_first(step)

    def reduce_z(it):
        def part(dz):
            mine = spread(bid(z + dz, y, c)) + cr[it, dz, y]
            if ny == 2:
                copy_ry(it, dz).wait_recv()
                mine = mine + yr[it, dz]
            return mine

        def step(dz):
            @pl.when(z + dz < nz)
            def _():
                zs[it, dz] = part(dz)
                copy_rz(it, dz, me + dz * plane).start()

        loop(1, nz, step)
        acc[...] = part(0)

    def reduce_finish(it):
        def step(dz):
            @pl.when(z >= dz)
            def _():
                copy_rz(it, dz, me).wait_recv()
                acc[...] += zr[it, dz]

        loop(1, nz, step)
        return acc[...]

    def reduce_drain(it):
        def step(dz):
            @pl.when(z + dz < nz)
            def _():
                copy_rc(it, dz).wait_send()
                if ny == 2:
                    copy_ry(it, dz).wait_send()

        loop(0, nz, step)

        def step_z(dz):
            @pl.when(z + dz < nz)
            def _():
                copy_rz(it, dz, me).wait_send()

        loop(1, nz, step_z)

    def copy_pp(i, k, slot, dev):
        ref = gp.at[i, slot]
        return remote(ref, ref, pps.at[i, k], ppr.at[i, k], dev)

    def sum_start(i, value):
        gp[i, me] = pack(value)
        loop(1, n, lambda k: copy_pp(i, k, me, peer(k)).start())

    def sum_finish(i):
        loop(1, n, lambda k: copy_pp(i, k, lax.rem(me - k + n, n), peer(k)).wait_recv())
        return unpack(jnp.sum(gp[i], axis=0))

    def sum_drain(i):
        loop(1, n, lambda k: copy_pp(i, k, me, peer(k)).wait_send())

    nr = rhs.shape[0]

    def product(x2, s, dims):
        both = fast(x2, bh[s], dims)
        return both[:nr] + both[nr:] + fast(x2[:nr], bl[s], dims)

    def split_block(s):
        load(s).wait()
        hi, lo = halves(stage[s])
        bh[s] = hi
        bl[s] = lo

    def mirror(x2, lo, hi):
        def step(s, carry):
            mir[s] = product(x2, s, NN)
            return carry

        lax.fori_loop(lo, hi, step, 0)

    def forward(it):
        def step(s, total):
            col = jnp.where(s < count, cols_ref[0, s], n)
            return total + product(stacked(gat[it, col]), s, NT)

        return lax.fori_loop(1, slots, step, zero)

    norm_part = exact(rhs, rhs, NT)
    pair = stacked(rhs)
    pl.semaphore_wait(barrier, n - 1)
    gather_start(0)
    sum_start(0, norm_part)

    def split_mirror(s, carry):
        split_block(s)
        mir[s] = product(pair, s, NN)
        return carry

    lax.fori_loop(1, 4, split_mirror, 0)
    gather_relay_z(0, 1)
    lax.fori_loop(4, 6, split_mirror, 0)
    gather_relay_z(0, 2)
    lax.fori_loop(6, slots, split_mirror, 0)
    loop(3, nz, lambda dz: gather_relay_z(0, dz))
    split_block(0)
    own0 = product(pair, 0, NT)
    gather_relay_y(0)
    reduce_core(0)
    reduce_y(0)
    gather_finish(0)
    fwd0 = forward(0)
    sum_start(1, exact(rhs, own0 + fwd0, NT) + exact(fwd0, rhs, NT))
    reduce_z(0)
    norm0 = sum_finish(0)
    alpha = solve_t(sum_finish(1), norm0)
    image0 = own0 + fwd0 + reduce_finish(0)
    residual = rhs - exact(alpha, image0)
    gat[1, me] = residual
    gather_start(1)
    sum_start(2, exact(residual, residual, NT))
    solution_t = exact(alpha, rhs)

    pair = stacked(residual)
    mirror(pair, 1, 4)
    gather_relay_z(1, 1)
    mirror(pair, 4, 6)
    gather_relay_z(1, 2)
    mirror(pair, 6, slots)
    loop(3, nz, lambda dz: gather_relay_z(1, dz))
    own1 = product(pair, 0, NT)
    norm1 = sum_finish(2)
    beta = solve_t(norm0, norm1)
    gather_relay_y(1)
    reduce_core(1)
    reduce_y(1)
    direction = residual + exact(beta, rhs)
    own_d = own1 + exact(beta, own0)
    turned0 = exact(beta, fwd0)
    image_d = own1 + exact(beta, image0)
    gather_finish(1)
    fwd1 = forward(1)
    fwd_d = fwd1 + turned0
    sum_start(3, exact(direction, own_d + fwd_d, NT) + exact(fwd_d, direction, NT))
    reduce_z(1)
    alpha = solve_t(sum_finish(3), norm1)
    image = image_d + fwd1 + reduce_finish(1)
    out_ref[0] = solution_t + exact(alpha, direction)
    out_ref[1] = residual - exact(alpha, image)

    for it in range(2):
        gather_drain(it)
        reduce_drain(it)
    for i in range(4):
        sum_drain(i)


def body(n, ny, right_side, blocks, block_cols, block_counts):
    width, nr = right_side.shape
    slots = blocks.shape[1]
    nz = n // (2 * ny)
    dma = pltpu.SemaphoreType.DMA
    vec = (nr, width)
    out = pl.pallas_call(
        functools.partial(kernel, n, ny),
        out_shape=jax.ShapeDtypeStruct((2,) + vec, F32),
        in_specs=[
            pl.BlockSpec(memory_space=pltpu.SMEM),
            pl.BlockSpec(memory_space=pltpu.SMEM),
            pl.BlockSpec(memory_space=pltpu.VMEM),
            pl.BlockSpec(memory_space=pl.ANY),
        ],
        out_specs=pl.BlockSpec(memory_space=pltpu.VMEM),
        scratch_shapes=[
            pltpu.VMEM((slots, width, width), F32),
            pltpu.VMEM((slots, width, width), BF16),
            pltpu.VMEM((slots, width, width), BF16),
            pltpu.VMEM((2, n + 1) + vec, F32),
            pltpu.VMEM((slots,) + vec, F32),
            pltpu.VMEM((2, nz, ny) + vec, F32),
            pltpu.VMEM((2, nz, ny) + vec, F32),
            pltpu.VMEM((2, nz if ny == 2 else 1) + vec, F32),
            pltpu.VMEM((2, nz if ny == 2 else 1) + vec, F32),
            pltpu.VMEM((2, nz) + vec, F32),
            pltpu.VMEM((2, nz) + vec, F32),
            pltpu.VMEM(vec, F32),
            pltpu.VMEM((4, n, 8, 4 * nr), F32),
            dma((slots,)),
            dma((2, nz)), dma((2, nz)),
            dma((2, nz if ny == 2 else 1)), dma((2, nz if ny == 2 else 1)),
            dma((2, nz * ny)), dma((2, nz * ny)),
            dma((2, nz)), dma((2, nz)),
            dma((2, nz if ny == 2 else 1)), dma((2, nz if ny == 2 else 1)),
            dma((2, nz)), dma((2, nz)),
            dma((4, n)), dma((4, n)),
        ],
        compiler_params=pltpu.CompilerParams(
            collective_id=0, has_side_effects=True, vmem_limit_bytes=58 * 2**20
        ),
    )(block_cols, block_counts, right_side.T, blocks)
    return out[0].T, out[1].T


def solution(mesh):
    in_specs = (
        P(("scen", "rb"), None),
        P(("scen", "rb"), None, None, None),
        P(("scen", "rb"), None),
        P(("scen", "rb")),
    )
    out_specs = (P(("scen", "rb"), None), P(("scen", "rb"), None))
    ny = max(1, 4 // mesh.shape["scen"])
    step = functools.partial(body, mesh.shape["rb"], ny)
    return jax.shard_map(step, mesh=mesh, in_specs=in_specs, out_specs=out_specs, check_vma=False)
```
